128 devices in a mesh: grid: 16 (over y, z_hi, core), band: 8 (over z_lo, x).
Axes of the slice: x: 4, y: 4, z: 4 (z_hi: 2, z_lo: 2; z = z_hi * 2 + z_lo), core: 2. Of those that a mesh axis runs over, the one named last changes fastest.
Arguments:
- orbitals: float32 [256, 96, 16, 128], P('band', 'grid'), may hold values from -6 to 6
- potential: float32 [96, 16, 128], P('grid'), may hold values from -2 to 0.5
- rotation: float32 [256, 256], replicated, may hold values from -0.375 to 0.375
Outputs:
- rotated: float32 [256, 96, 16, 128], P('band', 'grid')
The draws below stay inside these ranges and needn't reach their ends.
All inputs are finite; a program needn't handle non-finite values.
Results may differ from the reference program's by a relative error of at most 0.000071.
Values sent between devices are 32-bit elements; how exact they have to be, the bound alone decides.
A program may use at most 192 MiB of HBM per device.

```python
import jax
import jax.numpy as jnp
from jax import lax

NB = 256
DEGREE = 4
NY = 16
NZ = 128
NX = 96


def shard_levels(stream_key, shape, shards, low, largest):
    loudness, own = 1.0, jax.random.fold_in(stream_key, 6)
    for axis_at, shards_of in shards:
        heights = jnp.exp(jax.random.uniform(jax.random.fold_in(own, axis_at), (shards_of,), jnp.float32, low / len(shards), largest / len(shards)))
        loudness = loudness * jnp.repeat(heights, shape[axis_at] // shards_of).reshape([-1 if axis == axis_at else 1 for axis in range(len(shape))])
    return loudness


def bell_draw(own_key, extent, width, reach, cuts=(), dtype=jnp.bfloat16):
    values = width * jax.random.normal(own_key, extent, jnp.float32)
    if cuts:
        values = values * shard_levels(own_key, extent, cuts, -0.22, 0.18)
    return jnp.clip(values, -reach, reach).astype(dtype)


def setup_inputs(seed: int = 0) -> dict:
    keys = jax.random.split(jax.random.key(seed), 4)
    return {
        "orbitals": bell_draw(keys[0], (NB, NX, NY, NZ), 1.0, 6.0, ((0, 8), (1, 16)), jnp.float32),
        "potential": jnp.clip(-2.0 + 2.5 * jax.random.uniform(keys[1], (NX, NY, NZ), jnp.float32) ** shard_levels(keys[1], (NX, NY, NZ), ((0, 16),), -0.2, 0.2), -2.0, 0.5),
        "rotation": bell_draw(keys[2], (NB, NB), NB ** -0.5, 0.375, (), jnp.float32),
    }


stencil_coeffs = (12.0 / 7.0, -15.0 / 56.0, 10.0 / 189.0, -1.0 / 112.0, 2.0 / 1925.0, -1.0 / 16632.0)
centre_coeff = -5369.0 / 1800.0
bound_lower = -2.0
bound_cut = 1.0
bound_upper = 16.0


def apply_hamil(field, potential):
    laplace = 3.0 * centre_coeff * field
    for axis_num in range(3):
        for dist, coeff in enumerate(stencil_coeffs):
            laplace = laplace + coeff * (jnp.roll(field, dist + 1, axis=axis_num) + jnp.roll(field, -(dist + 1), axis=axis_num))
    return -0.5 * laplace + potential * field


def filter_one(orbital, potential):
    half_width = (bound_upper - bound_cut) / 2.0
    centre = (bound_upper + bound_cut) / 2.0
    sigma_first = half_width / (bound_lower - centre)
    sigma_now = sigma_first
    previous = orbital
    current = (apply_hamil(orbital, potential) - centre * orbital) * (sigma_first / half_width)
    for degree_step in range(DEGREE - 1):
        sigma_new = 1.0 / (2.0 / sigma_first - sigma_now)
        following = (2.0 * sigma_new / half_width) * (apply_hamil(current, potential) - centre * current) - (sigma_now * sigma_new) * previous
        previous = current
        current = following
        sigma_now = sigma_new
    return current


def reference(orbitals, potential, rotation):
    filtered = lax.map(lambda one: filter_one(one, potential), orbitals)
    return jnp.tensordot(rotation, filtered, axes=(0, 0), precision=lax.Precision.HIGHEST)
```

```python
import functools

import jax
import jax.numpy as jnp
from jax import lax
from jax.experimental import pallas as pl
from jax.experimental.pallas import tpu as pltpu
from jax.sharding import PartitionSpec as P

MESH = pl.DeviceIdType.MESH
DEGREE = 4
NB, NX, NY, NZ = 256, 96, 16, 128
GRID, BAND = 16, 8
SLAB = NX // GRID * NY
CELL = NX * NY
XL = 12
PAD = 6

stencil_coeffs = (12.0 / 7.0, -15.0 / 56.0, 10.0 / 189.0, -1.0 / 112.0, 2.0 / 1925.0, -1.0 / 16632.0)
centre_coeff = -5369.0 / 1800.0
bound_lower = -2.0
bound_cut = 1.0
bound_upper = 16.0
HALF = (bound_upper - bound_cut) / 2.0
CENTRE = (bound_upper + bound_cut) / 2.0


def step_factors():
    first = HALF / (bound_lower - CENTRE)
    now, out = first, [(first / HALF, 0.0)]
    for _ in range(DEGREE - 1):
        new = 1.0 / (2.0 / first - now)
        out.append((2.0 * new / HALF, now * new))
        now = new
    return out


def split(value):
    high = value.astype(jnp.bfloat16)
    return high, (value - high.astype(jnp.float32)).astype(jnp.bfloat16)


def tile_count(core, band):
    return 1 + (band + core) % 2


def tile_start(core, band):
    return 3 * (band // 2) + (band % 2) * (1 + core)


def kernel(orb, pot, rot, out, fin, fo, pbuf, w, e0, e1, mb, ob, rh, rl, cz,
           p_send, p_recv, s_send, s_recv, f_send, f_recv, m_send, m_recv, l_sem):
    g, b = lax.axis_index("grid"), lax.axis_index("band")
    y, zhi, core = g // 4, g // 2 % 2, g % 2
    zlo, x = b // 4, b % 4
    z = zhi * 2 + zlo
    cnt, first_tile = tile_count(core, b), tile_start(core, b)

    def grid_of(yy, zh, cc):
        return yy * 4 + zh * 2 + cc

    barrier = pltpu.get_barrier_semaphore()

    def greet(k, carry):
        t = lax.rem(g * BAND + b + k, GRID * BAND)
        pl.semaphore_signal(barrier, inc=1, device_id=(t // BAND, t % BAND), device_id_type=MESH)
        return carry

    lax.fori_loop(1, GRID * BAND, greet, 0)
    pl.semaphore_wait(barrier, GRID * BAND - 1)

    def pot_y(k, carry):
        pltpu.make_async_remote_copy(
            src_ref=pot, dst_ref=pbuf.at[y, zhi, core], send_sem=p_send.at[0], recv_sem=p_recv.at[0],
            device_id=(grid_of((y + 1 + (k + 1) % 3) % 4, zhi, core), b), device_id_type=MESH).start()
        return carry

    lax.fori_loop(0, 3, pot_y, 0)
    own_pot = pltpu.make_async_copy(pot, pbuf.at[y, zhi, core], l_sem.at[0])
    own_pot.start()

    def orb_out(h):
        def one(k, carry):
            dy, dz, dc = (2 + k // 4) % 4, 1 - k // 2 % 2, k % 2
            t = grid_of((y + dy) % 4, (zhi + dz) % 2, (core + dc) % 2)
            row = pl.multiple_of(g * SLAB, SLAB)

            @pl.when(k != 10)
            def _():
                pltpu.make_async_remote_copy(
                    src_ref=orb.at[h * GRID + t], dst_ref=fin.at[h, pl.ds(row, SLAB)],
                    send_sem=s_send.at[h], recv_sem=s_recv.at[h],
                    device_id=(t, b), device_id_type=MESH).start()

            @pl.when(k == 10)
            def _():
                pltpu.make_async_copy(
                    orb.at[h * GRID + g], fin.at[h, pl.ds(row, SLAB)], l_sem.at[1 + h]).start()
            return carry

        lax.fori_loop(0, GRID, one, 0)

    orb_out(0)

    own_pot.wait()
    three = pbuf.at[pl.ds(0, 3), 0, 0]
    pltpu.make_async_copy(three, three, p_recv.at[0]).wait()
    far = (grid_of(y, 1 - zhi, core), (1 - zlo) * 4 + x)
    copy2 = pltpu.make_async_remote_copy(
        src_ref=pbuf.at[:, zhi, core], dst_ref=pbuf.at[:, zhi, core],
        send_sem=p_send.at[1], recv_sem=p_recv.at[1], device_id=far, device_id_type=MESH)
    copy2.start()
    orb_out(1)

    turned = rot[...].T
    high, low = split(turned)
    rh[...] = high
    rl[...] = low
    row = lax.broadcasted_iota(jnp.int32, (NZ, NZ), 0)
    col = lax.broadcasted_iota(jnp.int32, (NZ, NZ), 1)
    away = jnp.abs(row - col)
    away = jnp.minimum(away, NZ - away)
    circ = jnp.zeros((NZ, NZ), jnp.float32)
    for dist, coeff in enumerate(stencil_coeffs):
        circ = jnp.where(away == dist + 1, -0.5 * coeff, circ)
    high, low = split(circ)
    cz[0:NZ, 0:NZ] = high
    cz[NZ:2 * NZ, 0:NZ] = high
    cz[0:NZ, NZ:2 * NZ] = low
    cz[NZ:2 * NZ, NZ:2 * NZ] = jnp.zeros((NZ, NZ), jnp.bfloat16)

    copy2.wait_recv()
    copy3 = pltpu.make_async_remote_copy(
        src_ref=pbuf.at[:, :, core], dst_ref=pbuf.at[:, :, core],
        send_sem=p_send.at[2], recv_sem=p_recv.at[2],
        device_id=(grid_of(y, zhi, 1 - core), b), device_id_type=MESH)
    copy3.start()
    copy3.wait_recv()
    flat = pbuf.reshape(CELL, NZ)

    def fill_w(xl, carry):
        for yy in range(NY):
            w[xl, yy] = flat[pl.ds(xl * NY + yy, 8, stride=XL * NY), :] - (CENTRE + 1.5 * centre_coeff)
        return carry

    lax.fori_loop(0, XL, fill_w, 0)

    def put(ref, xl, half, value):
        ref[xl + PAD] = value
        if half:
            ref[xl - PAD] = pltpu.roll(value, 1, 1)
        else:
            ref[xl + PAD + XL] = pltpu.roll(value, 7, 1)

    def hamil(src, xl):
        c = src[xl + PAD]
        high, low = split(c.reshape(NY * 8, NZ))
        zz = jnp.dot(jnp.concatenate([high, low], axis=1), cz[...], preferred_element_type=jnp.float32)
        acc = (zz[:, :NZ] + zz[:, NZ:]).reshape(NY, 8, NZ) + w[xl] * c
        for dist, coeff in enumerate(stencil_coeffs):
            d = dist + 1
            ring = jnp.concatenate([c[d:], c[:d]], axis=0) + jnp.concatenate([c[NY - d:], c[:NY - d]], axis=0)
            acc = acc + (-0.5 * coeff) * (ring + (src[xl + PAD + d] + src[xl + PAD - d]))
        return acc

    factors = step_factors()

    def one_band(h, carry):
        row = pl.multiple_of(g * SLAB, SLAB)
        pltpu.make_async_copy(orb.at[h * GRID + g], fin.at[h, pl.ds(row, SLAB)], l_sem.at[1 + h]).wait()
        most = fin.at[h, pl.ds(0, CELL - SLAB)]
        pltpu.make_async_copy(most, most, s_recv.at[h]).wait()
        landed, leave = fin.at[h], fo.at[h]
        for half in range(2):
            def load(i, c):
                xl = i + 6 * half
                rows = [landed[pl.ds(xl * NY + yy, 8, stride=XL * NY), :] for yy in range(NY)]
                put(e0, xl, half, jnp.stack(rows, axis=0))
                return c
            lax.fori_loop(0, 6, load, 0)
        for step, (a, prev) in enumerate(factors):
            src, dst = (e0, e1) if step % 2 == 0 else (e1, e0)
            for half in range(2):
                def plane(i, c):
                    xl = i + 6 * half
                    value = a * hamil(src, xl)
                    if step:
                        value = value - prev * dst[xl + PAD]
                    if step < DEGREE - 1:
                        put(dst, xl, half, value)
                    else:
                        for yy in range(NY):
                            leave[pl.ds(xl * NY + yy, 8, stride=XL * NY), :] = value[yy]
                    return c
                lax.fori_loop(0, 6, plane, 0)

        band_row = pl.multiple_of((32 * b + 16 * h + g) * 16, 16)
        for tile in range(2):
            def give(k, c):
                for dc in (1, 0):
                    yy, zz, xx = (y + 2 + k // 16) % 4, (z + 2 + k // 4) % 4, (x + 2 + k) % 4
                    cc, bb = (core + dc) % 2, zz % 2 * 4 + xx
                    gg = grid_of(yy, zz // 2, cc)
                    src_row = pl.multiple_of(gg * SLAB + (tile_start(cc, bb) + tile) * 8, 8)
                    send = pltpu.make_async_remote_copy(
                        src_ref=leave.at[pl.ds(src_row, 8)],
                        dst_ref=mb.at[pl.ds(pl.multiple_of(band_row + tile * 8, 8), 8)],
                        send_sem=f_send, recv_sem=f_recv.at[tile], device_id=(gg, bb), device_id_type=MESH)
                    wanted = tile_count(cc, bb) > tile if tile else True
                    if dc == 0:
                        wanted = jnp.logical_and(wanted, k != 42)
                    if wanted is True:
                        send.start()
                    else:
                        pl.when(wanted)(send.start)
                return c
            lax.fori_loop(0, 64, give, 0)

            def keep():
                own_row = pl.multiple_of(g * SLAB + (first_tile + tile) * 8, 8)
                own = pltpu.make_async_copy(
                    leave.at[pl.ds(own_row, 8)],
                    mb.at[pl.ds(pl.multiple_of(band_row + tile * 8, 8), 8)], l_sem.at[3])
                own.start()
                own.wait()
            if tile:
                pl.when(cnt > tile)(keep)
            else:
                keep()
        return carry

    lax.fori_loop(0, 2, one_band, 0)

    whole = mb.at[pl.ds(0, 254 * 8)]
    blocks = ob.reshape(NB, 16, NZ)

    def home(t):
        return pl.ds(pl.multiple_of((first_tile + t) * 8, 8), 8)

    def tile_work(tile):
        pltpu.make_async_copy(whole, whole, f_recv.at[tile]).wait()

        def pair(r, c):
            at = tile * 8 + 2 * r
            rows = [mb[pl.ds(at + i, NB, stride=16), :] for i in range(2)]
            high, low = split(jnp.concatenate(rows, axis=1))
            res = jnp.dot(rh[...], high, preferred_element_type=jnp.float32)
            res = res + (jnp.dot(rh[...], low, preferred_element_type=jnp.float32)
                         + jnp.dot(rl[...], high, preferred_element_type=jnp.float32))
            for i in range(2):
                ob[pl.ds(at + i, NB, stride=16), :] = res[:, i * NZ:(i + 1) * NZ]
            return c
        lax.fori_loop(0, 4, pair, 0)

        def give(k, c):
            t = lax.rem(b + k, BAND)
            pltpu.make_async_remote_copy(
                src_ref=blocks.at[pl.ds(t * 32, 32), pl.ds(tile * 8, 8)], dst_ref=out.at[:, home(tile)],
                send_sem=m_send, recv_sem=m_recv, device_id=(g, t), device_id_type=MESH).start()
            return c
        lax.fori_loop(1, BAND, give, 0)
        pltpu.make_async_copy(
            blocks.at[pl.ds(b * 32, 32), pl.ds(tile * 8, 8)], out.at[:, home(tile)], l_sem.at[4 + tile]).start()

    def own_done(tile):
        pltpu.make_async_copy(
            blocks.at[pl.ds(b * 32, 32), pl.ds(tile * 8, 8)], out.at[:, home(tile)], l_sem.at[4 + tile]).wait()

    tile_work(0)
    pl.when(cnt == 2)(lambda: tile_work(1))

    own_done(0)
    pl.when(cnt == 2)(lambda: own_done(1))
    for n in (1, 2):
        @pl.when(cnt == n)
        def _():
            got = out.at[:, pl.ds(0, (12 - n) * 8)]
            pltpu.make_async_copy(got, got, m_recv).wait()
            sent = blocks.at[pl.ds(0, 224), pl.ds(0, n * 8)]
            pltpu.make_async_copy(sent, sent, m_send).wait()
            sent = fo.at[:, pl.ds(0, (192 - n) * 8)]
            pltpu.make_async_copy(sent, sent, f_send).wait()
    pltpu.make_async_copy(three, three, p_send.at[0]).wait()
    copy2.wait_send()
    copy3.wait_send()
    for h in range(2):
        most = fin.at[h, pl.ds(0, CELL - SLAB)]
        pltpu.make_async_copy(most, most, s_send.at[h]).wait()


def local(orbitals, potential, rotation):
    bands = orbitals.shape[0]
    f32, bf16 = jnp.float32, jnp.bfloat16
    dma = pltpu.SemaphoreType.DMA
    result = pl.pallas_call(
        kernel,
        out_shape=jax.ShapeDtypeStruct((bands, SLAB, NZ), f32),
        in_specs=[pl.BlockSpec(memory_space=pltpu.HBM)] * 2 + [pl.BlockSpec(memory_space=pltpu.VMEM)],
        out_specs=pl.BlockSpec(memory_space=pltpu.HBM),
        scratch_shapes=[
            pltpu.VMEM((2, CELL, NZ), f32),
            pltpu.VMEM((2, CELL, NZ), f32),
            pltpu.VMEM((4, 2, 2, SLAB, NZ), f32),
            pltpu.VMEM((XL, NY, 8, NZ), f32),
            pltpu.VMEM((XL + 2 * PAD, NY, 8, NZ), f32),
            pltpu.VMEM((XL + 2 * PAD, NY, 8, NZ), f32),
            pltpu.VMEM((NB * 16, NZ), f32),
            pltpu.VMEM((NB * 16, NZ), f32),
            pltpu.VMEM((NB, NB), bf16),
            pltpu.VMEM((NB, NB), bf16),
            pltpu.VMEM((2 * NZ, 2 * NZ), bf16),
            dma((3,)), dma((3,)), dma((2,)), dma((2,)), dma, dma((2,)), dma, dma, dma((6,)),
        ],
        compiler_params=pltpu.CompilerParams(
            collective_id=0, has_side_effects=True, vmem_limit_bytes=48 * 2**20),
    )(orbitals.reshape(bands, SLAB, NZ), potential.reshape(SLAB, NZ), rotation)
    return result.reshape(orbitals.shape)


def solution(mesh):
    in_specs = (P("band", "grid", None, None), P("grid", None, None), P())
    out_specs = P("band", "grid", None, None)
    return jax.shard_map(local, mesh=mesh, in_specs=in_specs, out_specs=out_specs, check_vma=False)
```

```python
import functools

import jax
import jax.numpy as jnp
from jax import lax
from jax.experimental import pallas as pl
from jax.experimental.pallas import tpu as pltpu
from jax.sharding import PartitionSpec as P

MESH = pl.DeviceIdType.MESH
DEGREE = 4
NB, NX, NY, NZ = 256, 96, 16, 128
GRID, BAND = 16, 8
SLAB = NX // GRID * NY
CELL = NX * NY
XL = 12
PAD = 6
RUN = 3

stencil_coeffs = (12.0 / 7.0, -15.0 / 56.0, 10.0 / 189.0, -1.0 / 112.0, 2.0 / 1925.0, -1.0 / 16632.0)
centre_coeff = -5369.0 / 1800.0
bound_lower = -2.0
bound_cut = 1.0
bound_upper = 16.0
HALF = (bound_upper - bound_cut) / 2.0
CENTRE = (bound_upper + bound_cut) / 2.0


def step_factors():
    first = HALF / (bound_lower - CENTRE)
    now, out = first, [(first / HALF, 0.0)]
    for _ in range(DEGREE - 1):
        new = 1.0 / (2.0 / first - now)
        out.append((2.0 * new / HALF, now * new))
        now = new
    return out


def split(value):
    high = value.astype(jnp.bfloat16)
    return high, (value - high.astype(jnp.float32)).astype(jnp.bfloat16)


def tile_count(core, band):
    return 1 + (band + core) % 2


def tile_start(core, band):
    return 3 * (band // 2) + (band % 2) * (1 + core)


def kernel(orb, pot, rot, out, own, fin, fo, pbuf, w, e0, e1, mb, ob, rv, rh, rl, cz, ready,
           p_send, p_recv, s_send, s_recv, f_send, f_recv, m_send, m_recv, l_sem):
    g, b = lax.axis_index("grid"), lax.axis_index("band")
    y, zhi, core = g // 4, g // 2 % 2, g % 2
    zlo, x = b // 4, b % 4
    z = zhi * 2 + zlo
    cnt, first_tile = tile_count(core, b), tile_start(core, b)
    blocks, landing = ob.reshape(NB, 16, NZ), mb.reshape(NB, 16, NZ)

    def grid_of(yy, zh, cc):
        return yy * 4 + zh * 2 + cc

    orb_in = pltpu.make_async_copy(orb, own, l_sem.at[0])
    orb_in.start()
    pot_in = pltpu.make_async_copy(pot, pbuf.at[y, zhi, core], l_sem.at[1])
    pot_in.start()
    rot_in = pltpu.make_async_copy(rot, rv, l_sem.at[2])
    rot_in.start()

    far = (grid_of(y, 1 - zhi, core), (1 - zlo) * 4 + x)
    barrier = pltpu.get_barrier_semaphore()

    def greet_band(k, carry):
        pl.semaphore_signal(barrier, inc=1, device_id=(g, (b + k) % BAND), device_id_type=MESH)
        return carry

    def greet_grid(k, carry):
        pl.semaphore_signal(barrier, inc=1, device_id=((g + k) % GRID, b), device_id_type=MESH)
        return carry

    lax.fori_loop(1, BAND, greet_band, 0)
    lax.fori_loop(1, GRID, greet_grid, 0)
    pl.semaphore_signal(barrier, inc=1, device_id=far, device_id_type=MESH)
    pl.semaphore_wait(barrier, BAND + GRID - 1)

    def greet_all(k, carry):
        pl.semaphore_signal(ready, inc=1, device_id=(g, (b + k) % BAND), device_id_type=MESH)
        return carry

    orb_in.wait()

    def spread(tile):
        def one(k, carry):
            t = (zlo + 1 + k // 4) % 2 * 4 + (x + 2 + k) % 4
            rows = pl.ds(pl.multiple_of((tile_start(core, t) + tile) * 8, 8), 8)

            @pl.when(jnp.logical_and(k != 6, tile_count(core, t) > tile))
            def _():
                pltpu.make_async_remote_copy(
                    src_ref=own.at[:, rows], dst_ref=landing.at[pl.ds(b * 32, 32), pl.ds(tile * 8, 8)],
                    send_sem=s_send, recv_sem=s_recv.at[tile], device_id=(g, t), device_id_type=MESH).start()
            return carry

        lax.fori_loop(0, BAND, one, 0)

    def mine(tile):
        rows = pl.ds(pl.multiple_of((first_tile + tile) * 8, 8), 8)
        return pltpu.make_async_copy(
            own.at[:, rows], landing.at[pl.ds(b * 32, 32), pl.ds(tile * 8, 8)], l_sem.at[3 + tile])

    spread(0)
    mine(0).start()
    spread(1)
    pl.when(cnt == 2)(lambda: mine(1).start())
    lax.fori_loop(1, BAND, greet_all, 0)

    pot_in.wait()

    def pot_y(k, carry):
        pltpu.make_async_remote_copy(
            src_ref=pbuf.at[y, zhi, core], dst_ref=pbuf.at[y, zhi, core],
            send_sem=p_send.at[0], recv_sem=p_recv.at[0],
            device_id=(grid_of((y + 1 + (k + 1) % 3) % 4, zhi, core), b), device_id_type=MESH).start()
        return carry

    lax.fori_loop(0, 3, pot_y, 0)

    rot_in.wait()
    high, low = split(rv[...].T)
    rh[...] = high
    rl[...] = low
    row = lax.broadcasted_iota(jnp.int32, (NZ, NZ), 0)
    col = lax.broadcasted_iota(jnp.int32, (NZ, NZ), 1)
    away = jnp.abs(row - col)
    away = jnp.minimum(away, NZ - away)
    circ = jnp.zeros((NZ, NZ), jnp.float32)
    for dist, coeff in enumerate(stencil_coeffs):
        circ = jnp.where(away == dist + 1, -0.5 * coeff, circ)
    high, low = split(circ)
    cz[0:NZ, 0:NZ] = high
    cz[NZ:2 * NZ, 0:NZ] = high
    cz[0:NZ, NZ:2 * NZ] = low
    cz[NZ:2 * NZ, NZ:2 * NZ] = jnp.zeros((NZ, NZ), jnp.bfloat16)

    three = pbuf.at[pl.ds(0, 3), 0, 0]
    pltpu.make_async_copy(three, three, p_recv.at[0]).wait()
    copy2 = pltpu.make_async_remote_copy(
        src_ref=pbuf.at[:, zhi, core], dst_ref=pbuf.at[:, zhi, core],
        send_sem=p_send.at[1], recv_sem=p_recv.at[1], device_id=far, device_id_type=MESH)
    copy2.start()
    copy2.wait_recv()
    copy3 = pltpu.make_async_remote_copy(
        src_ref=pbuf.at[:, :, core], dst_ref=pbuf.at[:, :, core],
        send_sem=p_send.at[2], recv_sem=p_recv.at[2],
        device_id=(grid_of(y, zhi, 1 - core), b), device_id_type=MESH)
    copy3.start()
    pl.semaphore_wait(ready, BAND - 1)

    def rotate(tile):
        mine(tile).wait()
        got = landing.at[pl.ds(0, NB - 32), pl.ds(0, 8)]
        pltpu.make_async_copy(got, got, s_recv.at[tile]).wait()

        def pair(r, c):
            at = tile * 8 + 2 * r
            rows = [mb[pl.ds(at + i, NB, stride=16), :] for i in range(2)]
            high, low = split(jnp.concatenate(rows, axis=1))
            res = jnp.dot(rh[...], high, preferred_element_type=jnp.float32)
            res = res + (jnp.dot(rh[...], low, preferred_element_type=jnp.float32)
                         + jnp.dot(rl[...], high, preferred_element_type=jnp.float32))
            for i in range(2):
                ob[pl.ds(at + i, NB, stride=16), :] = res[:, i * NZ:(i + 1) * NZ]
            return c
        lax.fori_loop(0, 4, pair, 0)

    def gather(h, tile, tiles):
        place = pl.ds(pl.multiple_of(g * SLAB + (first_tile + tile) * 8, 8), 8 * tiles)

        def rows(gg, bb):
            return ob.at[pl.ds(pl.multiple_of((32 * bb + 16 * h + gg) * 16 + tile * 8, 8), 8 * tiles)]

        def one(k, c):
            for dc in (1, 0):
                yy, zz, xx = (y + 2 + k // 16) % 4, (z + 2 + k // 4) % 4, (x + 2 + k) % 4
                gg, bb = grid_of(yy, zz // 2, (core + dc) % 2), zz % 2 * 4 + xx
                send = pltpu.make_async_remote_copy(
                    src_ref=rows(gg, bb), dst_ref=fin.at[h, place],
                    send_sem=m_send, recv_sem=m_recv.at[h], device_id=(gg, bb), device_id_type=MESH)
                if dc == 0:
                    pl.when(k != 42)(send.start)
                else:
                    send.start()
            return c
        lax.fori_loop(0, 64, one, 0)
        keep = pltpu.make_async_copy(rows(g, b), fin.at[h, place], l_sem.at[5])
        keep.start()
        keep.wait()

    rotate(0)
    gather(0, 0, 1)

    @pl.when(cnt == 2)
    def _():
        rotate(1)
        gather(0, 1, 1)
        gather(1, 0, 2)

    @pl.when(cnt == 1)
    def _():
        gather(1, 0, 1)

    copy3.wait_recv()
    flat = pbuf.reshape(CELL, NZ)

    def fill_w(xl, carry):
        for yy in range(NY):
            w[xl, yy] = flat[pl.ds(xl * NY + yy, 8, stride=XL * NY), :] - (CENTRE + 1.5 * centre_coeff)
        return carry

    lax.fori_loop(0, XL, fill_w, 0)

    def put(ref, xl, half, value):
        ref[xl + PAD] = value
        if half:
            ref[xl - PAD] = pltpu.roll(value, 1, 1)
        else:
            ref[xl + PAD + XL] = pltpu.roll(value, 7, 1)

    def stencil_xy(src, xl):
        c = src[xl + PAD]
        acc = w[xl] * c
        for dist, coeff in enumerate(stencil_coeffs):
            d = dist + 1
            ring = jnp.concatenate([c[d:], c[:d]], axis=0) + jnp.concatenate([c[NY - d:], c[:NY - d]], axis=0)
            acc = acc + (-0.5 * coeff) * (ring + (src[xl + PAD + d] + src[xl + PAD - d]))
        return acc

    def stencil_z(src, xl):
        high, low = split(src[pl.ds(xl + PAD, RUN)].reshape(RUN * NY * 8, NZ))
        both = jnp.dot(jnp.concatenate([high, low], axis=1), cz[...], preferred_element_type=jnp.float32)
        return (both[:, :NZ] + both[:, NZ:]).reshape(RUN, NY, 8, NZ)

    factors = step_factors()

    def one_band(h, carry):
        for n in (1, 2):
            @pl.when(cnt == n)
            def _():
                most = fin.at[h, pl.ds(0, (192 - n) * 8)]
                pltpu.make_async_copy(most, most, m_recv.at[h]).wait()
        landed, leave = fin.at[h], fo.at[h]
        for half in range(2):
            def load(i, c):
                xl = i + 6 * half
                rows = [landed[pl.ds(xl * NY + yy, 8, stride=XL * NY), :] for yy in range(NY)]
                put(e0, xl, half, jnp.stack(rows, axis=0))
                return c
            lax.fori_loop(0, 6, load, 0)
        for step, (a, prev) in enumerate(factors):
            src, dst = (e0, e1) if step % 2 == 0 else (e1, e0)
            for half in range(2):
                def planes(i, c):
                    along_z = stencil_z(src, i * RUN + 6 * half)
                    for j in range(RUN):
                        xl = i * RUN + j + 6 * half
                        value = a * (stencil_xy(src, xl) + along_z[j])
                        if step:
                            value = value - prev * dst[xl + PAD]
                        if step < DEGREE - 1:
                            put(dst, xl, half, value)
                        else:
                            for yy in range(NY):
                                leave[pl.ds(xl * NY + yy, 8, stride=XL * NY), :] = value[yy]
                    return c
                lax.fori_loop(0, 6 // RUN, planes, 0)

        def home(k, c):
            dy, dz, dc = (2 + k // 4) % 4, 1 - k // 2 % 2, k % 2
            t = grid_of((y + dy) % 4, (zhi + dz) % 2, (core + dc) % 2)
            slab = leave.at[pl.ds(pl.multiple_of(t * SLAB, SLAB), SLAB)]

            @pl.when(k != 10)
            def _():
                pltpu.make_async_remote_copy(
                    src_ref=slab, dst_ref=out.at[h * GRID + g], send_sem=f_send, recv_sem=f_recv,
                    device_id=(t, b), device_id_type=MESH).start()

            @pl.when(k == 10)
            def _():
                pltpu.make_async_copy(slab, out.at[h * GRID + g], l_sem.at[6 + h]).start()
            return c
        lax.fori_loop(0, GRID, home, 0)
        return carry

    lax.fori_loop(0, 2, one_band, 0)

    for h in range(2):
        slab = fo.at[h, pl.ds(pl.multiple_of(g * SLAB, SLAB), SLAB)]
        pltpu.make_async_copy(slab, out.at[h * GRID + g], l_sem.at[6 + h]).wait()
    got = out.at[pl.ds(0, 2 * GRID - 2)]
    pltpu.make_async_copy(got, got, f_recv).wait()
    pltpu.make_async_copy(got, got, f_send).wait()
    for n in (1, 2):
        @pl.when(cnt == n)
        def _():
            sent = own.at[:, pl.ds(0, (12 - n) * 8)]
            pltpu.make_async_copy(sent, sent, s_send).wait()
            sent = mb.at[pl.ds(0, 254 * 8 * n)]
            pltpu.make_async_copy(sent, sent, m_send).wait()
    pltpu.make_async_copy(three, three, p_send.at[0]).wait()
    copy2.wait_send()
    copy3.wait_send()


def local(orbitals, potential, rotation):
    bands = orbitals.shape[0]
    f32, bf16 = jnp.float32, jnp.bfloat16
    dma = pltpu.SemaphoreType.DMA
    result = pl.pallas_call(
        kernel,
        out_shape=jax.ShapeDtypeStruct((bands, SLAB, NZ), f32),
        in_specs=[pl.BlockSpec(memory_space=pltpu.HBM)] * 3,
        out_specs=pl.BlockSpec(memory_space=pltpu.HBM),
        scratch_shapes=[
            pltpu.VMEM((bands, SLAB, NZ), f32),
            pltpu.VMEM((2, CELL, NZ), f32),
            pltpu.VMEM((2, CELL, NZ), f32),
            pltpu.VMEM((4, 2, 2, SLAB, NZ), f32),
            pltpu.VMEM((XL, NY, 8, NZ), f32),
            pltpu.VMEM((XL + 2 * PAD, NY, 8, NZ), f32),
            pltpu.VMEM((XL + 2 * PAD, NY, 8, NZ), f32),
            pltpu.VMEM((NB * 16, NZ), f32),
            pltpu.VMEM((NB * 16, NZ), f32),
            pltpu.VMEM((NB, NB), f32),
            pltpu.VMEM((NB, NB), bf16),
            pltpu.VMEM((NB, NB), bf16),
            pltpu.VMEM((2 * NZ, 2 * NZ), bf16),
            pltpu.SemaphoreType.REGULAR,
            dma((3,)), dma((3,)), dma, dma((2,)), dma, dma, dma, dma((2,)), dma((8,)),
        ],
        compiler_params=pltpu.CompilerParams(
            collective_id=0, has_side_effects=True, vmem_limit_bytes=62 * 2**20),
    )(orbitals.reshape(bands, SLAB, NZ), potential.reshape(SLAB, NZ), rotation)
    return result.reshape(orbitals.shape)


def solution(mesh):
    in_specs = (P("band", "grid", None, None), P("grid", None, None), P())
    out_specs = P("band", "grid", None, None)
    return jax.shard_map(local, mesh=mesh, in_specs=in_specs, out_specs=out_specs, check_vma=False)
```

```python
import functools

import jax
import jax.numpy as jnp
from jax import lax
from jax.experimental import pallas as pl
from jax.experimental.pallas import tpu as pltpu
from jax.sharding import PartitionSpec as P

MESH = pl.DeviceIdType.MESH
DEGREE = 4
NB, NX, NY, NZ = 256, 96, 16, 128
GRID, BAND = 16, 8
SLAB = NX // GRID * NY
CELL = NX * NY
XL = 12
PAD = 6
RUN = 6

stencil_coeffs = (12.0 / 7.0, -15.0 / 56.0, 10.0 / 189.0, -1.0 / 112.0, 2.0 / 1925.0, -1.0 / 16632.0)
centre_coeff = -5369.0 / 1800.0
bound_lower = -2.0
bound_cut = 1.0
bound_upper = 16.0
HALF = (bound_upper - bound_cut) / 2.0
CENTRE = (bound_upper + bound_cut) / 2.0


def step_factors():
    first = HALF / (bound_lower - CENTRE)
    now, out = first, [(first / HALF, 0.0)]
    for _ in range(DEGREE - 1):
        new = 1.0 / (2.0 / first - now)
        out.append((2.0 * new / HALF, now * new))
        now = new
    return out


def split(value):
    high = value.astype(jnp.bfloat16)
    return high, (value - high.astype(jnp.float32)).astype(jnp.bfloat16)


def tile_count(core, band):
    return 1 + (band + core) % 2


def tile_start(core, band):
    return 3 * (band // 2) + (band % 2) * (1 + core)


def kernel(orb, pot, rot, out, own, fin, fo, pbuf, w, e0, e1, mb, ob, rv, rh, rl, cz, ready,
           p_send, p_recv, s_send, s_recv, f_send, f_recv, m_send, m_recv, l_sem):
    g, b = lax.axis_index("grid"), lax.axis_index("band")
    y, zhi, core = g // 4, g // 2 % 2, g % 2
    zlo, x = b // 4, b % 4
    z = zhi * 2 + zlo
    cnt, first_tile = tile_count(core, b), tile_start(core, b)
    blocks, landing = ob.reshape(NB, 16, NZ), mb.reshape(NB, 16, NZ)

    def grid_of(yy, zh, cc):
        return yy * 4 + zh * 2 + cc

    orb_in = pltpu.make_async_copy(orb, own, l_sem.at[0])
    orb_in.start()
    pot_in = pltpu.make_async_copy(pot, pbuf.at[y, zhi, core], l_sem.at[1])
    pot_in.start()
    rot_in = pltpu.make_async_copy(rot, rv, l_sem.at[2])
    rot_in.start()

    far = (grid_of(y, 1 - zhi, core), (1 - zlo) * 4 + x)
    barrier = pltpu.get_barrier_semaphore()

    def greet_band(k, carry):
        pl.semaphore_signal(barrier, inc=1, device_id=(g, (b + k) % BAND), device_id_type=MESH)
        return carry

    def greet_grid(k, carry):
        pl.semaphore_signal(barrier, inc=1, device_id=((g + k) % GRID, b), device_id_type=MESH)
        return carry

    lax.fori_loop(1, BAND, greet_band, 0)
    lax.fori_loop(1, GRID, greet_grid, 0)
    pl.semaphore_signal(barrier, inc=1, device_id=far, device_id_type=MESH)
    pl.semaphore_wait(barrier, BAND + GRID - 1)

    def greet_all(k, carry):
        pl.semaphore_signal(ready, inc=1, device_id=(g, (b + k) % BAND), device_id_type=MESH)
        return carry

    orb_in.wait()

    def spread(tile):
        def one(k, carry):
            t = (zlo + 1 + k // 4) % 2 * 4 + (x + 2 + k) % 4
            rows = pl.ds(pl.multiple_of((tile_start(core, t) + tile) * 8, 8), 8)

            @pl.when(jnp.logical_and(k != 6, tile_count(core, t) > tile))
            def _():
                pltpu.make_async_remote_copy(
                    src_ref=own.at[:, rows], dst_ref=landing.at[pl.ds(b * 32, 32), pl.ds(tile * 8, 8)],
                    send_sem=s_send, recv_sem=s_recv.at[tile], device_id=(g, t), device_id_type=MESH).start()
            return carry

        lax.fori_loop(0, BAND, one, 0)

    def mine(tile):
        rows = pl.ds(pl.multiple_of((first_tile + tile) * 8, 8), 8)
        return pltpu.make_async_copy(
            own.at[:, rows], landing.at[pl.ds(b * 32, 32), pl.ds(tile * 8, 8)], l_sem.at[3 + tile])

    spread(0)
    mine(0).start()
    spread(1)
    pl.when(cnt == 2)(lambda: mine(1).start())
    lax.fori_loop(1, BAND, greet_all, 0)

    pot_in.wait()

    def pot_y(k, carry):
        pltpu.make_async_remote_copy(
            src_ref=pbuf.at[y, zhi, core], dst_ref=pbuf.at[y, zhi, core],
            send_sem=p_send.at[0], recv_sem=p_recv.at[0],
            device_id=(grid_of((y + 1 + (k + 1) % 3) % 4, zhi, core), b), device_id_type=MESH).start()
        return carry

    lax.fori_loop(0, 3, pot_y, 0)

    rot_in.wait()
    high, low = split(rv[...].T)
    rh[...] = high
    rl[...] = low
    row = lax.broadcasted_iota(jnp.int32, (NZ, NZ), 0)
    col = lax.broadcasted_iota(jnp.int32, (NZ, NZ), 1)
    away = jnp.abs(row - col)
    away = jnp.minimum(away, NZ - away)
    circ = jnp.zeros((NZ, NZ), jnp.float32)
    for dist, coeff in enumerate(stencil_coeffs):
        circ = jnp.where(away == dist + 1, -0.5 * coeff, circ)
    high, low = split(circ)
    cz[0:NZ, 0:NZ] = high
    cz[NZ:2 * NZ, 0:NZ] = high
    cz[0:NZ, NZ:2 * NZ] = low
    cz[NZ:2 * NZ, NZ:2 * NZ] = jnp.zeros((NZ, NZ), jnp.bfloat16)

    three = pbuf.at[pl.ds(0, 3), 0, 0]
    pltpu.make_async_copy(three, three, p_recv.at[0]).wait()
    copy2 = pltpu.make_async_remote_copy(
        src_ref=pbuf.at[:, zhi, core], dst_ref=pbuf.at[:, zhi, core],
        send_sem=p_send.at[1], recv_sem=p_recv.at[1], device_id=far, device_id_type=MESH)
    copy2.start()
    copy2.wait_recv()
    copy3 = pltpu.make_async_remote_copy(
        src_ref=pbuf.at[:, :, core], dst_ref=pbuf.at[:, :, core],
        send_sem=p_send.at[2], recv_sem=p_recv.at[2],
        device_id=(grid_of(y, zhi, 1 - core), b), device_id_type=MESH)
    copy3.start()
    copy3.wait_recv()
    flat = pbuf.reshape(CELL, NZ)

    def fill_w(xl, carry):
        for yy in range(NY):
            w[xl, yy] = flat[pl.ds(xl * NY + yy, 8, stride=XL * NY), :] - (CENTRE + 1.5 * centre_coeff)
        return carry

    lax.fori_loop(0, XL, fill_w, 0)

    pl.semaphore_wait(ready, BAND - 1)

    def rotate(tile):
        mine(tile).wait()
        got = landing.at[pl.ds(0, NB - 32), pl.ds(0, 8)]
        pltpu.make_async_copy(got, got, s_recv.at[tile]).wait()

        def pair(r, c):
            at = tile * 8 + 2 * r
            rows = [mb[pl.ds(at + i, NB, stride=16), :] for i in range(2)]
            high, low = split(jnp.concatenate(rows, axis=1))
            res = jnp.dot(rh[...], high, preferred_element_type=jnp.float32)
            res = res + (jnp.dot(rh[...], low, preferred_element_type=jnp.float32)
                         + jnp.dot(rl[...], high, preferred_element_type=jnp.float32))
            for i in range(2):
                ob[pl.ds(at + i, NB, stride=16), :] = res[:, i * NZ:(i + 1) * NZ]
            return c
        lax.fori_loop(0, 4, pair, 0)

    def gather(h, tile, tiles):
        place = pl.ds(pl.multiple_of(g * SLAB + (first_tile + tile) * 8, 8), 8 * tiles)

        def rows(gg, bb):
            return ob.at[pl.ds(pl.multiple_of((32 * bb + 16 * h + gg) * 16 + tile * 8, 8), 8 * tiles)]

        def one(first, c, k):
            for dc in (1, 0):
                xy = k // 2 if first == 1 else k
                dz = (2, 1 + 2 * (k % 2), 0)[first]
                yy, zz, xx = (y + 2 + xy // 4) % 4, (z + dz) % 4, (x + 2 + xy + xy // 4) % 4
                gg, bb = grid_of(yy, zz // 2, (core + dc) % 2), zz % 2 * 4 + xx
                send = pltpu.make_async_remote_copy(
                    src_ref=rows(gg, bb), dst_ref=fin.at[h, place],
                    send_sem=m_send.at[h], recv_sem=m_recv.at[h], device_id=(gg, bb), device_id_type=MESH)
                if dc == 0 and first == 2:
                    pl.when(k != 8)(send.start)
                else:
                    send.start()
            return c
        for first, count in enumerate((16, 32, 16)):
            lax.fori_loop(0, count, lambda k, c: one(first, c, k), 0)
        keep = pltpu.make_async_copy(rows(g, b), fin.at[h, place], l_sem.at[5])
        keep.start()
        keep.wait()

    def sent_all(h, n):
        sent = mb.at[pl.ds(0, 127 * 8 * n)]
        pltpu.make_async_copy(sent, sent, m_send.at[h]).wait()

    rotate(0)
    gather(0, 0, 1)

    @pl.when(cnt == 2)
    def _():
        rotate(1)
        gather(0, 1, 1)
        sent_all(0, 2)
        gather(1, 0, 2)

    @pl.when(cnt == 1)
    def _():
        sent_all(0, 1)
        gather(1, 0, 1)

    def put(ref, xl, half, value):
        ref[xl + PAD] = value
        if half:
            ref[xl - PAD] = pltpu.roll(value, 1, 1)
        else:
            ref[xl + PAD + XL] = pltpu.roll(value, 7, 1)

    def stencil_xy(src, xl):
        c = src[xl + PAD]
        acc = w[xl] * c
        for dist, coeff in enumerate(stencil_coeffs):
            d = dist + 1
            ring = jnp.concatenate([c[d:], c[:d]], axis=0) + jnp.concatenate([c[NY - d:], c[:NY - d]], axis=0)
            acc = acc + (-0.5 * coeff) * (ring + (src[xl + PAD + d] + src[xl + PAD - d]))
        return acc

    def stencil_z(src, xl):
        high, low = split(src[pl.ds(xl + PAD, RUN)].reshape(RUN * NY * 8, NZ))
        both = jnp.dot(jnp.concatenate([high, low], axis=1), cz[...], preferred_element_type=jnp.float32)
        return (both[:, :NZ] + both[:, NZ:]).reshape(RUN, NY, 8, NZ)

    factors = step_factors()

    def home(h, first, last):
        def one(k, c):
            dy, dz, dc = (2 + k // 2 % 4) % 4, 1 - k % 2, 1 - k // 8
            t = grid_of((y + dy) % 4, (zhi + dz) % 2, (core + dc) % 2)
            slab = fo.at[h, pl.ds(pl.multiple_of(t * SLAB, SLAB), SLAB)]

            @pl.when(k != 13)
            def _():
                pltpu.make_async_remote_copy(
                    src_ref=slab, dst_ref=out.at[h * GRID + g], send_sem=f_send, recv_sem=f_recv,
                    device_id=(t, b), device_id_type=MESH).start()

            @pl.when(k == 13)
            def _():
                pltpu.make_async_copy(slab, out.at[h * GRID + g], l_sem.at[6 + h]).start()
            return c
        lax.fori_loop(first, last, one, 0)

    def one_band(h, carry):
        for n in (1, 2):
            @pl.when(cnt == n)
            def _():
                most = fin.at[h, pl.ds(0, (192 - n) * 8)]
                pltpu.make_async_copy(most, most, m_recv.at[h]).wait()

        @pl.when(h == 1)
        def _():
            home(0, 8, 16)

        landed, leave = fin.at[h], fo.at[h]
        for half in range(2):
            def load(i, c):
                xl = i + 6 * half
                rows = [landed[pl.ds(xl * NY + yy, 8, stride=XL * NY), :] for yy in range(NY)]
                put(e0, xl, half, jnp.stack(rows, axis=0))
                return c
            lax.fori_loop(0, 6, load, 0)
        for step, (a, prev) in enumerate(factors):
            src, dst = (e0, e1) if step % 2 == 0 else (e1, e0)
            for half in range(2):
                def planes(i, c):
                    along_z = stencil_z(src, i * RUN + 6 * half)
                    for j in range(RUN):
                        xl = i * RUN + j + 6 * half
                        value = a * (stencil_xy(src, xl) + along_z[j])
                        if step:
                            value = value - prev * dst[xl + PAD]
                        if step < DEGREE - 1:
                            put(dst, xl, half, value)
                        else:
                            for yy in range(NY):
                                leave[pl.ds(xl * NY + yy, 8, stride=XL * NY), :] = value[yy]
                    return c
                lax.fori_loop(0, 6 // RUN, planes, 0)


        @pl.when(h == 0)
        def _():
            home(0, 0, 8)
        return carry

    lax.fori_loop(0, 2, one_band, 0)
    home(1, 0, GRID)

    for h in range(2):
        slab = fo.at[h, pl.ds(pl.multiple_of(g * SLAB, SLAB), SLAB)]
        pltpu.make_async_copy(slab, out.at[h * GRID + g], l_sem.at[6 + h]).wait()
    got = out.at[pl.ds(0, 2 * GRID - 2)]
    pltpu.make_async_copy(got, got, f_recv).wait()
    pltpu.make_async_copy(got, got, f_send).wait()
    for n in (1, 2):
        @pl.when(cnt == n)
        def _():
            sent = own.at[:, pl.ds(0, (12 - n) * 8)]
            pltpu.make_async_copy(sent, sent, s_send).wait()
            sent_all(1, n)
    pltpu.make_async_copy(three, three, p_send.at[0]).wait()
    copy2.wait_send()
    copy3.wait_send()


def local(orbitals, potential, rotation):
    bands = orbitals.shape[0]
    f32, bf16 = jnp.float32, jnp.bfloat16
    dma = pltpu.SemaphoreType.DMA
    arrays = orbitals.reshape(bands, SLAB, NZ), potential.reshape(SLAB, NZ), rotation
    result = pl.pallas_call(
        kernel,
        out_shape=jax.ShapeDtypeStruct((bands, SLAB, NZ), f32),
        in_specs=[pl.BlockSpec(memory_space=pltpu.HBM)] * 3,
        out_specs=pl.BlockSpec(memory_space=pltpu.HBM),
        scratch_shapes=[
            pltpu.VMEM((bands, SLAB, NZ), f32),
            pltpu.VMEM((2, CELL, NZ), f32),
            pltpu.VMEM((2, CELL, NZ), f32),
            pltpu.VMEM((4, 2, 2, SLAB, NZ), f32),
            pltpu.VMEM((XL, NY, 8, NZ), f32),
            pltpu.VMEM((XL + 2 * PAD, NY, 8, NZ), f32),
            pltpu.VMEM((XL + 2 * PAD, NY, 8, NZ), f32),
            pltpu.VMEM((NB * 16, NZ), f32),
            pltpu.VMEM((NB * 16, NZ), f32),
            pltpu.VMEM((NB, NB), f32),
            pltpu.VMEM((NB, NB), bf16),
            pltpu.VMEM((NB, NB), bf16),
            pltpu.VMEM((2 * NZ, 2 * NZ), bf16),
            pltpu.SemaphoreType.REGULAR,
            dma((3,)), dma((3,)), dma, dma((2,)), dma, dma, dma((2,)), dma((2,)), dma((8,)),
        ],
        compiler_params=pltpu.CompilerParams(
            collective_id=0, has_side_effects=True, vmem_limit_bytes=40 * 2**20),
    )(*[pltpu.with_memory_space_constraint(value, pltpu.HBM) for value in arrays])
    return result.reshape(orbitals.shape)


def solution(mesh):
    in_specs = (P("band", "grid", None, None), P("grid", None, None), P())
    out_specs = P("band", "grid", None, None)
    return jax.shard_map(local, mesh=mesh, in_specs=in_specs, out_specs=out_specs, check_vma=False)
```

```python
import functools

import jax
import jax.numpy as jnp
from jax import lax
from jax.experimental import pallas as pl
from jax.experimental.pallas import tpu as pltpu
from jax.sharding import PartitionSpec as P

MESH = pl.DeviceIdType.MESH
DEGREE = 4
NB, NX, NY, NZ = 256, 96, 16, 128
GRID, BAND = 16, 8
SLAB = NX // GRID * NY
CELL = NX * NY
XL = 12
PAD = 6
RUN = 6

stencil_coeffs = (12.0 / 7.0, -15.0 / 56.0, 10.0 / 189.0, -1.0 / 112.0, 2.0 / 1925.0, -1.0 / 16632.0)
centre_coeff = -5369.0 / 1800.0
bound_lower = -2.0
bound_cut = 1.0
bound_upper = 16.0
HALF = (bound_upper - bound_cut) / 2.0
CENTRE = (bound_upper + bound_cut) / 2.0


def step_factors():
    first = HALF / (bound_lower - CENTRE)
    now, out = first, [(first / HALF, 0.0)]
    for _ in range(DEGREE - 1):
        new = 1.0 / (2.0 / first - now)
        out.append((2.0 * new / HALF, now * new))
        now = new
    return out


def split(value):
    high = value.astype(jnp.bfloat16)
    return high, (value - high.astype(jnp.float32)).astype(jnp.bfloat16)


def tile_count(core, band):
    return 1 + (band + core) % 2


def tile_start(core, band):
    return 3 * (band // 2) + (band % 2) * (1 + core)


def kernel(orb, pot, rot, out, own, fin, fo, pbuf, w, e0, e1, mb, ob, rv, rh, rl, cz, ready,
           p_send, p_recv, s_send, s_recv, f_send, f_recv, m_send, m_recv, l_sem):
    g, b = lax.axis_index("grid"), lax.axis_index("band")
    y, zhi, core = g // 4, g // 2 % 2, g % 2
    zlo, x = b // 4, b % 4
    z = zhi * 2 + zlo
    cnt, first_tile = tile_count(core, b), tile_start(core, b)
    blocks, landing = ob.reshape(NB, 16, NZ), mb.reshape(NB, 16, NZ)

    def grid_of(yy, zh, cc):
        return yy * 4 + zh * 2 + cc

    orb_in = pltpu.make_async_copy(orb, own, l_sem.at[0])
    orb_in.start()
    pot_in = pltpu.make_async_copy(pot, pbuf.at[y, zhi, core], l_sem.at[1])
    pot_in.start()
    rot_in = pltpu.make_async_copy(rot, rv, l_sem.at[2])
    rot_in.start()

    far = (grid_of(y, 1 - zhi, core), (1 - zlo) * 4 + x)
    barrier = pltpu.get_barrier_semaphore()

    def greet_band(k, carry):
        pl.semaphore_signal(barrier, inc=1, device_id=(g, (b + k) % BAND), device_id_type=MESH)
        return carry

    def greet_grid(k, carry):
        pl.semaphore_signal(barrier, inc=1, device_id=((g + k) % GRID, b), device_id_type=MESH)
        return carry

    lax.fori_loop(1, BAND, greet_band, 0)
    lax.fori_loop(1, GRID, greet_grid, 0)
    pl.semaphore_signal(barrier, inc=1, device_id=far, device_id_type=MESH)
    pl.semaphore_wait(barrier, BAND + GRID - 1)

    def greet_all(k, carry):
        pl.semaphore_signal(ready, inc=1, device_id=(g, (b + k) % BAND), device_id_type=MESH)
        return carry

    orb_in.wait()

    def spread(tile):
        def one(k, carry):
            t = (zlo + 1 + k // 4) % 2 * 4 + (x + 2 + k) % 4
            rows = pl.ds(pl.multiple_of((tile_start(core, t) + tile) * 8, 8), 8)

            @pl.when(jnp.logical_and(k != 6, tile_count(core, t) > tile))
            def _():
                pltpu.make_async_remote_copy(
                    src_ref=own.at[:, rows], dst_ref=landing.at[pl.ds(b * 32, 32), pl.ds(tile * 8, 8)],
                    send_sem=s_send, recv_sem=s_recv.at[tile], device_id=(g, t), device_id_type=MESH).start()
            return carry

        lax.fori_loop(0, BAND, one, 0)

    def mine(tile):
        rows = pl.ds(pl.multiple_of((first_tile + tile) * 8, 8), 8)
        return pltpu.make_async_copy(
            own.at[:, rows], landing.at[pl.ds(b * 32, 32), pl.ds(tile * 8, 8)], l_sem.at[3 + tile])

    spread(0)
    mine(0).start()
    spread(1)
    pl.when(cnt == 2)(lambda: mine(1).start())
    lax.fori_loop(1, BAND, greet_all, 0)

    pot_in.wait()

    def pot_y(k, carry):
        pltpu.make_async_remote_copy(
            src_ref=pbuf.at[y, zhi, core], dst_ref=pbuf.at[y, zhi, core],
            send_sem=p_send.at[0], recv_sem=p_recv.at[0],
            device_id=(grid_of((y + 1 + (k + 1) % 3) % 4, zhi, core), b), device_id_type=MESH).start()
        return carry

    lax.fori_loop(0, 3, pot_y, 0)

    rot_in.wait()
    high, low = split(rv[...].T)
    rh[...] = high
    rl[...] = low
    row = lax.broadcasted_iota(jnp.int32, (NZ, NZ), 0)
    col = lax.broadcasted_iota(jnp.int32, (NZ, NZ), 1)
    away = jnp.abs(row - col)
    away = jnp.minimum(away, NZ - away)
    circ = jnp.zeros((NZ, NZ), jnp.float32)
    for dist, coeff in enumerate(stencil_coeffs):
        circ = jnp.where(away == dist + 1, -0.5 * coeff, circ)
    high, low = split(circ)
    cz[0:NZ, 0:NZ] = high
    cz[NZ:2 * NZ, 0:NZ] = high
    cz[0:NZ, NZ:2 * NZ] = low
    cz[NZ:2 * NZ, NZ:2 * NZ] = jnp.zeros((NZ, NZ), jnp.bfloat16)

    three = pbuf.at[pl.ds(0, 3), 0, 0]
    pltpu.make_async_copy(three, three, p_recv.at[0]).wait()
    copy2 = pltpu.make_async_remote_copy(
        src_ref=pbuf.at[:, zhi, core], dst_ref=pbuf.at[:, zhi, core],
        send_sem=p_send.at[1], recv_sem=p_recv.at[1], device_id=far, device_id_type=MESH)
    copy2.start()
    copy2.wait_recv()
    copy3 = pltpu.make_async_remote_copy(
        src_ref=pbuf.at[:, :, core], dst_ref=pbuf.at[:, :, core],
        send_sem=p_send.at[2], recv_sem=p_recv.at[2],
        device_id=(grid_of(y, zhi, 1 - core), b), device_id_type=MESH)
    copy3.start()
    copy3.wait_recv()
    flat = pbuf.reshape(CELL, NZ)

    def fill_w(xl, carry):
        for yy in range(NY):
            w[xl, yy] = flat[pl.ds(xl * NY + yy, 8, stride=XL * NY), :] - (CENTRE + 1.5 * centre_coeff)
        return carry

    lax.fori_loop(0, XL, fill_w, 0)

    pl.semaphore_wait(ready, BAND - 1)

    def rotate(tile):
        mine(tile).wait()
        got = landing.at[pl.ds(0, NB - 32), pl.ds(0, 8)]
        pltpu.make_async_copy(got, got, s_recv.at[tile]).wait()

        def pair(r, c):
            at = tile * 8 + 2 * r
            rows = [mb[pl.ds(at + i, NB, stride=16), :] for i in range(2)]
            high, low = split(jnp.concatenate(rows, axis=1))
            res = jnp.dot(rh[...], high, preferred_element_type=jnp.float32)
            res = res + (jnp.dot(rh[...], low, preferred_element_type=jnp.float32)
                         + jnp.dot(rl[...], high, preferred_element_type=jnp.float32))
            for i in range(2):
                ob[pl.ds(at + i, NB, stride=16), :] = res[:, i * NZ:(i + 1) * NZ]
            return c
        lax.fori_loop(0, 4, pair, 0)

    def gather(h, tile, tiles):
        place = pl.ds(pl.multiple_of(g * SLAB + (first_tile + tile) * 8, 8), 8 * tiles)

        def rows(gg, bb):
            return ob.at[pl.ds(pl.multiple_of((32 * bb + 16 * h + gg) * 16 + tile * 8, 8), 8 * tiles)]

        def one(first, c, k):
            for dc in (1, 0):
                xy = k // 2 if first == 1 else k
                dz = (2, 1 + 2 * (k % 2), 0)[first]
                yy, zz, xx = (y + 2 + xy // 4) % 4, (z + dz) % 4, (x + 2 + xy + xy // 4) % 4
                gg, bb = grid_of(yy, zz // 2, (core + dc) % 2), zz % 2 * 4 + xx
                send = pltpu.make_async_remote_copy(
                    src_ref=rows(gg, bb), dst_ref=fin.at[h, place],
                    send_sem=m_send.at[h], recv_sem=m_recv.at[h], device_id=(gg, bb), device_id_type=MESH)
                if dc == 0 and first == 2:
                    pl.when(k != 8)(send.start)
                else:
                    send.start()
            return c
        for first, count in enumerate((16, 32, 16)):
            lax.fori_loop(0, count, lambda k, c: one(first, c, k), 0)
        keep = pltpu.make_async_copy(rows(g, b), fin.at[h, place], l_sem.at[5])
        keep.start()
        keep.wait()

    def sent_all(h, n):
        sent = mb.at[pl.ds(0, 127 * 8 * n)]
        pltpu.make_async_copy(sent, sent, m_send.at[h]).wait()

    rotate(0)
    gather(0, 0, 1)

    @pl.when(cnt == 2)
    def _():
        rotate(1)
        gather(0, 1, 1)
        sent_all(0, 2)
        gather(1, 0, 2)

    @pl.when(cnt == 1)
    def _():
        sent_all(0, 1)
        gather(1, 0, 1)

    def put(ref, xl, half, value):
        ref[xl + PAD] = value
        if half:
            ref[xl - PAD] = pltpu.roll(value, 1, 1)
        else:
            ref[xl + PAD + XL] = pltpu.roll(value, 7, 1)

    def stencil_xy(src, xl):
        c = src[xl + PAD]
        acc = w[xl] * c
        for dist, coeff in enumerate(stencil_coeffs):
            d = dist + 1
            ring = jnp.concatenate([c[d:], c[:d]], axis=0) + jnp.concatenate([c[NY - d:], c[:NY - d]], axis=0)
            acc = acc + (-0.5 * coeff) * (ring + (src[xl + PAD + d] + src[xl + PAD - d]))
        return acc

    def stencil_z(src, xl):
        high, low = split(src[pl.ds(xl + PAD, RUN)].reshape(RUN * NY * 8, NZ))
        both = jnp.dot(jnp.concatenate([high, low], axis=1), cz[...], preferred_element_type=jnp.float32)
        return (both[:, :NZ] + both[:, NZ:]).reshape(RUN, NY, 8, NZ)

    factors = step_factors()

    def home(h, first, last):
        def one(k, c):
            dy, dz, dc = (2 + k // 2 % 4) % 4, 1 - k % 2, 1 - k // 8
            t = grid_of((y + dy) % 4, (zhi + dz) % 2, (core + dc) % 2)
            slab = fo.at[h, pl.ds(pl.multiple_of(t * SLAB, SLAB), SLAB)]

            @pl.when(k != 13)
            def _():
                pltpu.make_async_remote_copy(
                    src_ref=slab, dst_ref=out.at[h * GRID + g], send_sem=f_send, recv_sem=f_recv,
                    device_id=(t, b), device_id_type=MESH).start()

            @pl.when(k == 13)
            def _():
                pltpu.make_async_copy(slab, out.at[h * GRID + g], l_sem.at[6 + h]).start()
            return c
        lax.fori_loop(first, last, one, 0)

    def one_band(h, carry):
        for n in (1, 2):
            @pl.when(cnt == n)
            def _():
                most = fin.at[h, pl.ds(0, (192 - n) * 8)]
                pltpu.make_async_copy(most, most, m_recv.at[h]).wait()

        @pl.when(h == 1)
        def _():
            home(0, 8 * core, 8 * core + 8)

        landed, leave = fin.at[h], fo.at[h]
        for half in range(2):
            def load(i, c):
                xl = i + 6 * half
                rows = [landed[pl.ds(xl * NY + yy, 8, stride=XL * NY), :] for yy in range(NY)]
                put(e0, xl, half, jnp.stack(rows, axis=0))
                return c
            lax.fori_loop(0, 6, load, 0)
        for step, (a, prev) in enumerate(factors):
            src, dst = (e0, e1) if step % 2 == 0 else (e1, e0)
            for half in range(2):
                def planes(i, c):
                    along_z = stencil_z(src, i * RUN + 6 * half)
                    for j in range(RUN):
                        xl = i * RUN + j + 6 * half
                        value = a * (stencil_xy(src, xl) + along_z[j])
                        if step:
                            value = value - prev * dst[xl + PAD]
                        if step < DEGREE - 1:
                            put(dst, xl, half, value)
                        else:
                            for yy in range(NY):
                                leave[pl.ds(xl * NY + yy, 8, stride=XL * NY), :] = value[yy]
                    return c
                lax.fori_loop(0, 6 // RUN, planes, 0)
                if step == DEGREE - 1 and half == 0:
                    home(h, 8 - 8 * core, 16 - 8 * core)

        return carry

    lax.fori_loop(0, 2, one_band, 0)
    home(1, 8 * core, 8 * core + 8)

    for h in range(2):
        slab = fo.at[h, pl.ds(pl.multiple_of(g * SLAB, SLAB), SLAB)]
        pltpu.make_async_copy(slab, out.at[h * GRID + g], l_sem.at[6 + h]).wait()
    got = out.at[pl.ds(0, 2 * GRID - 2)]
    pltpu.make_async_copy(got, got, f_recv).wait()
    pltpu.make_async_copy(got, got, f_send).wait()
    for n in (1, 2):
        @pl.when(cnt == n)
        def _():
            sent = own.at[:, pl.ds(0, (12 - n) * 8)]
            pltpu.make_async_copy(sent, sent, s_send).wait()
            sent_all(1, n)
    pltpu.make_async_copy(three, three, p_send.at[0]).wait()
    copy2.wait_send()
    copy3.wait_send()


def local(orbitals, potential, rotation):
    bands = orbitals.shape[0]
    f32, bf16 = jnp.float32, jnp.bfloat16
    dma = pltpu.SemaphoreType.DMA
    arrays = orbitals.reshape(bands, SLAB, NZ), potential.reshape(SLAB, NZ), rotation
    result = pl.pallas_call(
        kernel,
        out_shape=jax.ShapeDtypeStruct((bands, SLAB, NZ), f32),
        in_specs=[pl.BlockSpec(memory_space=pltpu.HBM)] * 3,
        out_specs=pl.BlockSpec(memory_space=pltpu.HBM),
        scratch_shapes=[
            pltpu.VMEM((bands, SLAB, NZ), f32),
            pltpu.VMEM((2, CELL, NZ), f32),
            pltpu.VMEM((2, CELL, NZ), f32),
            pltpu.VMEM((4, 2, 2, SLAB, NZ), f32),
            pltpu.VMEM((XL, NY, 8, NZ), f32),
            pltpu.VMEM((XL + 2 * PAD, NY, 8, NZ), f32),
            pltpu.VMEM((XL + 2 * PAD, NY, 8, NZ), f32),
            pltpu.VMEM((NB * 16, NZ), f32),
            pltpu.VMEM((NB * 16, NZ), f32),
            pltpu.VMEM((NB, NB), f32),
            pltpu.VMEM((NB, NB), bf16),
            pltpu.VMEM((NB, NB), bf16),
            pltpu.VMEM((2 * NZ, 2 * NZ), bf16),
            pltpu.SemaphoreType.REGULAR,
            dma((3,)), dma((3,)), dma, dma((2,)), dma, dma, dma((2,)), dma((2,)), dma((8,)),
        ],
        compiler_params=pltpu.CompilerParams(
            collective_id=0, has_side_effects=True, vmem_limit_bytes=40 * 2**20),
    )(*[pltpu.with_memory_space_constraint(value, pltpu.HBM) for value in arrays])
    return result.reshape(orbitals.shape)


def solution(mesh):
    in_specs = (P("band", "grid", None, None), P("grid", None, None), P())
    out_specs = P("band", "grid", None, None)
    return jax.shard_map(local, mesh=mesh, in_specs=in_specs, out_specs=out_specs, check_vma=False)
```

```python
import functools

import jax
import jax.numpy as jnp
from jax import lax
from jax.experimental import pallas as pl
from jax.experimental.pallas import tpu as pltpu
from jax.sharding import PartitionSpec as P

MESH = pl.DeviceIdType.MESH
DEGREE = 4
NB, NX, NY, NZ = 256, 96, 16, 128
GRID, BAND = 16, 8
SLAB = NX // GRID * NY
CELL = NX * NY
XL = 12
PAD = 6
RUN = 6

stencil_coeffs = (12.0 / 7.0, -15.0 / 56.0, 10.0 / 189.0, -1.0 / 112.0, 2.0 / 1925.0, -1.0 / 16632.0)
centre_coeff = -5369.0 / 1800.0
bound_lower = -2.0
bound_cut = 1.0
bound_upper = 16.0
HALF = (bound_upper - bound_cut) / 2.0
CENTRE = (bound_upper + bound_cut) / 2.0


def step_factors():
    first = HALF / (bound_lower - CENTRE)
    now, out = first, [(first / HALF, 0.0)]
    for _ in range(DEGREE - 1):
        new = 1.0 / (2.0 / first - now)
        out.append((2.0 * new / HALF, now * new))
        now = new
    return out


def split(value):
    high = value.astype(jnp.bfloat16)
    return high, (value - high.astype(jnp.float32)).astype(jnp.bfloat16)


def tile_count(core, band):
    return 1 + (band + core) % 2


def tile_start(core, band):
    return 3 * (band // 2) + (band % 2) * (1 + core)


def kernel(orb, pot, rot, out, own, fin, fo, pbuf, w, e0, e1, mb, ob, rv, rh, rl, cz, ready,
           p_send, p_recv, s_send, s_recv, f_send, f_recv, m_send, m_recv, l_sem):
    g, b = lax.axis_index("grid"), lax.axis_index("band")
    y, zhi, core = g // 4, g // 2 % 2, g % 2
    zlo, x = b // 4, b % 4
    z = zhi * 2 + zlo
    cnt, first_tile = tile_count(core, b), tile_start(core, b)
    blocks, landing = ob.reshape(NB, 16, NZ), mb.reshape(NB, 16, NZ)

    def grid_of(yy, zh, cc):
        return yy * 4 + zh * 2 + cc

    orb_in = pltpu.make_async_copy(orb, own, l_sem.at[0])
    orb_in.start()
    pot_in = pltpu.make_async_copy(pot, pbuf.at[y, zhi, core], l_sem.at[1])
    pot_in.start()
    rot_in = pltpu.make_async_copy(rot, rv, l_sem.at[2])
    rot_in.start()

    far = (grid_of(y, 1 - zhi, core), (1 - zlo) * 4 + x)
    barrier = pltpu.get_barrier_semaphore()

    def greet_band(k, carry):
        pl.semaphore_signal(barrier, inc=1, device_id=(g, (b + k) % BAND), device_id_type=MESH)
        return carry

    def greet_grid(k, carry):
        pl.semaphore_signal(barrier, inc=1, device_id=((g + k) % GRID, b), device_id_type=MESH)
        return carry

    lax.fori_loop(1, BAND, greet_band, 0)
    lax.fori_loop(1, GRID, greet_grid, 0)
    pl.semaphore_signal(barrier, inc=1, device_id=far, device_id_type=MESH)
    pl.semaphore_wait(barrier, BAND + GRID - 1)

    def greet_all(k, carry):
        pl.semaphore_signal(ready, inc=1, device_id=(g, (b + k) % BAND), device_id_type=MESH)
        return carry

    orb_in.wait()

    def spread(tile):
        def one(k, carry):
            t = (zlo + 1 + k // 4) % 2 * 4 + (x + 2 + k) % 4
            rows = pl.ds(pl.multiple_of((tile_start(core, t) + tile) * 8, 8), 8)

            @pl.when(jnp.logical_and(k != 6, tile_count(core, t) > tile))
            def _():
                pltpu.make_async_remote_copy(
                    src_ref=own.at[:, rows], dst_ref=landing.at[pl.ds(b * 32, 32), pl.ds(tile * 8, 8)],
                    send_sem=s_send, recv_sem=s_recv.at[tile], device_id=(g, t), device_id_type=MESH).start()
            return carry

        lax.fori_loop(0, BAND, one, 0)

    def mine(tile):
        rows = pl.ds(pl.multiple_of((first_tile + tile) * 8, 8), 8)
        return pltpu.make_async_copy(
            own.at[:, rows], landing.at[pl.ds(b * 32, 32), pl.ds(tile * 8, 8)], l_sem.at[3 + tile])

    spread(0)
    mine(0).start()
    spread(1)
    pl.when(cnt == 2)(lambda: mine(1).start())
    lax.fori_loop(1, BAND, greet_all, 0)

    pot_in.wait()

    def pot_y(k, carry):
        pltpu.make_async_remote_copy(
            src_ref=pbuf.at[y, zhi, core], dst_ref=pbuf.at[y, zhi, core],
            send_sem=p_send.at[0], recv_sem=p_recv.at[0],
            device_id=(grid_of((y + 1 + (k + 1) % 3) % 4, zhi, core), b), device_id_type=MESH).start()
        return carry

    lax.fori_loop(0, 3, pot_y, 0)

    rot_in.wait()
    high, low = split(rv[...].T)
    rh[...] = high
    rl[...] = low
    row = lax.broadcasted_iota(jnp.int32, (NZ, NZ), 0)
    col = lax.broadcasted_iota(jnp.int32, (NZ, NZ), 1)
    away = jnp.abs(row - col)
    away = jnp.minimum(away, NZ - away)
    circ = jnp.zeros((NZ, NZ), jnp.float32)
    for dist, coeff in enumerate(stencil_coeffs):
        circ = jnp.where(away == dist + 1, -0.5 * coeff, circ)
    high, low = split(circ)
    cz[0:NZ, 0:NZ] = high
    cz[NZ:2 * NZ, 0:NZ] = high
    cz[0:NZ, NZ:2 * NZ] = low
    cz[NZ:2 * NZ, NZ:2 * NZ] = jnp.zeros((NZ, NZ), jnp.bfloat16)

    three = pbuf.at[pl.ds(0, 3), 0, 0]
    pltpu.make_async_copy(three, three, p_recv.at[0]).wait()
    copy2 = pltpu.make_async_remote_copy(
        src_ref=pbuf.at[:, zhi, core], dst_ref=pbuf.at[:, zhi, core],
        send_sem=p_send.at[1], recv_sem=p_recv.at[1], device_id=far, device_id_type=MESH)
    copy2.start()
    copy2.wait_recv()
    copy3 = pltpu.make_async_remote_copy(
        src_ref=pbuf.at[:, :, core], dst_ref=pbuf.at[:, :, core],
        send_sem=p_send.at[2], recv_sem=p_recv.at[2],
        device_id=(grid_of(y, zhi, 1 - core), b), device_id_type=MESH)
    copy3.start()
    copy3.wait_recv()
    flat = pbuf.reshape(CELL, NZ)

    def fill_w(xl, carry):
        for yy in range(NY):
            w[xl, yy] = flat[pl.ds(xl * NY + yy, 8, stride=XL * NY), :] - (CENTRE + 1.5 * centre_coeff)
        return carry

    lax.fori_loop(0, XL, fill_w, 0)

    pl.semaphore_wait(ready, BAND - 1)

    def rotate(tile):
        mine(tile).wait()
        got = landing.at[pl.ds(0, NB - 32), pl.ds(0, 8)]
        pltpu.make_async_copy(got, got, s_recv.at[tile]).wait()

        def pair(r, c):
            at = tile * 8 + 2 * r
            rows = [mb[pl.ds(at + i, NB, stride=16), :] for i in range(2)]
            high, low = split(jnp.concatenate(rows, axis=1))
            res = jnp.dot(rh[...], high, preferred_element_type=jnp.float32)
            res = res + (jnp.dot(rh[...], low, preferred_element_type=jnp.float32)
                         + jnp.dot(rl[...], high, preferred_element_type=jnp.float32))
            for i in range(2):
                ob[pl.ds(at + i, NB, stride=16), :] = res[:, i * NZ:(i + 1) * NZ]
            return c
        lax.fori_loop(0, 4, pair, 0)

    def gather(h, tile, tiles):
        place = pl.ds(pl.multiple_of(g * SLAB + (first_tile + tile) * 8, 8), 8 * tiles)

        def rows(gg, bb):
            return ob.at[pl.ds(pl.multiple_of((32 * bb + 16 * h + gg) * 16 + tile * 8, 8), 8 * tiles)]

        def one(first, c, k):
            for dc in (1, 0):
                xy = k // 2 if first == 1 else k
                dz = (2, 1 + 2 * (k % 2), 0)[first]
                yy, zz, xx = (y + 2 + xy // 4) % 4, (z + dz) % 4, (x + 2 + xy + xy // 4) % 4
                gg, bb = grid_of(yy, zz // 2, (core + dc) % 2), zz % 2 * 4 + xx
                send = pltpu.make_async_remote_copy(
                    src_ref=rows(gg, bb), dst_ref=fin.at[h, place],
                    send_sem=m_send.at[h], recv_sem=m_recv.at[h], device_id=(gg, bb), device_id_type=MESH)
                if dc == 0 and first == 2:
                    pl.when(k != 8)(send.start)
                else:
                    send.start()
            return c
        for first, count in enumerate((16, 32, 16)):
            lax.fori_loop(0, count, lambda k, c: one(first, c, k), 0)
        keep = pltpu.make_async_copy(rows(g, b), fin.at[h, place], l_sem.at[(5 + 3 * tile) if h == 0 else 9])
        keep.start()
        return keep

    def sent_all(h, n):
        sent = mb.at[pl.ds(0, 127 * 8 * n)]
        pltpu.make_async_copy(sent, sent, m_send.at[h]).wait()

    rotate(0)
    kept = gather(0, 0, 1)

    @pl.when(cnt == 2)
    def _():
        rotate(1)
        more = gather(0, 1, 1)
        sent_all(0, 2)
        gather(1, 0, 2).wait()
        more.wait()

    @pl.when(cnt == 1)
    def _():
        sent_all(0, 1)
        gather(1, 0, 1).wait()

    kept.wait()

    def put(ref, xl, half, value):
        ref[xl + PAD] = value
        if half:
            ref[xl - PAD] = pltpu.roll(value, 1, 1)
        else:
            ref[xl + PAD + XL] = pltpu.roll(value, 7, 1)

    def stencil_xy(src, xl):
        c = src[xl + PAD]
        acc = w[xl] * c
        for dist, coeff in enumerate(stencil_coeffs):
            d = dist + 1
            ring = jnp.concatenate([c[d:], c[:d]], axis=0) + jnp.concatenate([c[NY - d:], c[:NY - d]], axis=0)
            acc = acc + (-0.5 * coeff) * (ring + (src[xl + PAD + d] + src[xl + PAD - d]))
        return acc

    def stencil_z(src, xl):
        high, low = split(src[pl.ds(xl + PAD, RUN)].reshape(RUN * NY * 8, NZ))
        both = jnp.dot(jnp.concatenate([high, low], axis=1), cz[...], preferred_element_type=jnp.float32)
        return (both[:, :NZ] + both[:, NZ:]).reshape(RUN, NY, 8, NZ)

    factors = step_factors()

    def home(h, first, last):
        def one(k, c):
            dy, dz, dc = (2 + k // 2 % 4) % 4, 1 - k % 2, 1 - k // 8
            t = grid_of((y + dy) % 4, (zhi + dz) % 2, (core + dc) % 2)
            slab = fo.at[h, pl.ds(pl.multiple_of(t * SLAB, SLAB), SLAB)]

            @pl.when(k != 13)
            def _():
                pltpu.make_async_remote_copy(
                    src_ref=slab, dst_ref=out.at[h * GRID + g], send_sem=f_send, recv_sem=f_recv,
                    device_id=(t, b), device_id_type=MESH).start()

            @pl.when(k == 13)
            def _():
                pltpu.make_async_copy(slab, out.at[h * GRID + g], l_sem.at[6 + h]).start()
            return c
        lax.fori_loop(first, last, one, 0)

    def one_band(h, carry):
        for n in (1, 2):
            @pl.when(cnt == n)
            def _():
                most = fin.at[h, pl.ds(0, (192 - n) * 8)]
                pltpu.make_async_copy(most, most, m_recv.at[h]).wait()

        @pl.when(h == 1)
        def _():
            home(0, 8 * core, 8 * core + 8)

        landed, leave = fin.at[h], fo.at[h]
        for half in range(2):
            def load(i, c):
                xl = i + 6 * half
                rows = [landed[pl.ds(xl * NY + yy, 8, stride=XL * NY), :] for yy in range(NY)]
                put(e0, xl, half, jnp.stack(rows, axis=0))
                return c
            lax.fori_loop(0, 6, load, 0)
        for step, (a, prev) in enumerate(factors):
            src, dst = (e0, e1) if step % 2 == 0 else (e1, e0)
            for half in range(2):
                def planes(i, c):
                    along_z = stencil_z(src, i * RUN + 6 * half)
                    for j in range(RUN):
                        xl = i * RUN + j + 6 * half
                        value = a * (stencil_xy(src, xl) + along_z[j])
                        if step:
                            value = value - prev * dst[xl + PAD]
                        if step < DEGREE - 1:
                            put(dst, xl, half, value)
                        else:
                            for yy in range(NY):
                                leave[pl.ds(xl * NY + yy, 8, stride=XL * NY), :] = value[yy]
                    return c
                lax.fori_loop(0, 6 // RUN, planes, 0)
                if step == DEGREE - 1 and half == 0:
                    home(h, 8 - 8 * core, 16 - 8 * core)

        return carry

    lax.fori_loop(0, 2, one_band, 0)
    home(1, 8 * core, 8 * core + 8)

    for h in range(2):
        slab = fo.at[h, pl.ds(pl.multiple_of(g * SLAB, SLAB), SLAB)]
        pltpu.make_async_copy(slab, out.at[h * GRID + g], l_sem.at[6 + h]).wait()
    got = out.at[pl.ds(0, 2 * GRID - 2)]
    pltpu.make_async_copy(got, got, f_recv).wait()
    pltpu.make_async_copy(got, got, f_send).wait()
    for n in (1, 2):
        @pl.when(cnt == n)
        def _():
            sent = own.at[:, pl.ds(0, (12 - n) * 8)]
            pltpu.make_async_copy(sent, sent, s_send).wait()
            sent_all(1, n)
    pltpu.make_async_copy(three, three, p_send.at[0]).wait()
    copy2.wait_send()
    copy3.wait_send()


def local(orbitals, potential, rotation):
    bands = orbitals.shape[0]
    f32, bf16 = jnp.float32, jnp.bfloat16
    dma = pltpu.SemaphoreType.DMA
    arrays = orbitals.reshape(bands, SLAB, NZ), potential.reshape(SLAB, NZ), rotation
    result = pl.pallas_call(
        kernel,
        out_shape=jax.ShapeDtypeStruct((bands, SLAB, NZ), f32),
        in_specs=[pl.BlockSpec(memory_space=pltpu.HBM)] * 3,
        out_specs=pl.BlockSpec(memory_space=pltpu.HBM),
        scratch_shapes=[
            pltpu.VMEM((bands, SLAB, NZ), f32),
            pltpu.VMEM((2, CELL, NZ), f32),
            pltpu.VMEM((2, CELL, NZ), f32),
            pltpu.VMEM((4, 2, 2, SLAB, NZ), f32),
            pltpu.VMEM((XL, NY, 8, NZ), f32),
            pltpu.VMEM((XL + 2 * PAD, NY, 8, NZ), f32),
            pltpu.VMEM((XL + 2 * PAD, NY, 8, NZ), f32),
            pltpu.VMEM((NB * 16, NZ), f32),
            pltpu.VMEM((NB * 16, NZ), f32),
            pltpu.VMEM((NB, NB), f32),
            pltpu.VMEM((NB, NB), bf16),
            pltpu.VMEM((NB, NB), bf16),
            pltpu.VMEM((2 * NZ, 2 * NZ), bf16),
            pltpu.SemaphoreType.REGULAR,
            dma((3,)), dma((3,)), dma, dma((2,)), dma, dma, dma((2,)), dma((2,)), dma((10,)),
        ],
        compiler_params=pltpu.CompilerParams(
            collective_id=0, has_side_effects=True, vmem_limit_bytes=40 * 2**20),
    )(*[pltpu.with_memory_space_constraint(value, pltpu.HBM) for value in arrays])
    return result.reshape(orbitals.shape)


def solution(mesh):
    in_specs = (P("band", "grid", None, None), P("grid", None, None), P())
    out_specs = P("band", "grid", None, None)
    return jax.shard_map(local, mesh=mesh, in_specs=in_specs, out_specs=out_specs, check_vma=False)
```
